32 devices in a mesh: lat: 8 (over z, y), lon: 4 (over x, core).
Axes of the slice: x: 2, y: 2, z: 4, core: 2. Of those that a mesh axis runs over, the one named last changes fastest.
Arguments:
- views: bfloat16 [2, 32, 192, 4096], P(None, 'lat', None, 'lon'), may hold values from -8 to 8
- conv_weight: bfloat16 [9, 192, 192], replicated, may hold values from -0.15625 to 0.15625
- match_weight: bfloat16 [128, 192], replicated, may hold values from -0.4375 to 0.4375
- value_weight: bfloat16 [128, 192], replicated, may hold values from -0.4375 to 0.4375
- post_gain: float32 [128], replicated, may hold values from 0.1 to 1.9
- out_weight: bfloat16 [192, 128], replicated, may hold values from -0.5 to 0.5
Outputs:
- coded_maps: bfloat16 [2, 32, 192, 4096], P(None, 'lat', None, 'lon')
The draws below stay inside these ranges and needn't reach their ends.
All inputs are finite; a program needn't handle non-finite values.
Results may differ from the reference program's by a relative error of at most 0.0054.
Values may be sent and summed in bfloat16 or wider, within the bound.
A program may use at most 320 MiB of HBM per device.

```python
import jax
import jax.numpy as jnp
from jax import lax

C = 192
A = 128
W = 4096
ROWS = 32


def draw_views(key, part):
    return jnp.clip(jax.random.normal(key, (2, ROWS, C, W), jnp.float32), -8.0, 8.0).astype(jnp.bfloat16)


def normal_values(rng, shape, width, most, kind=jnp.bfloat16):
    drawn = jax.random.normal(rng, shape, jnp.float32) * width
    return jnp.minimum(jnp.maximum(drawn, -most), most).astype(kind)


def setup_inputs(seed: int = 0) -> dict:
    keys = jax.random.split(jax.random.key(seed), 7)
    views = draw_views(jax.random.fold_in(keys[6], 71), 0)
    conv_weight = normal_values(keys[1], (9, C, C), (9 * C) ** -0.5, 0.15625)
    match_weight = normal_values(keys[2], (A, C), C ** -0.5, 0.4375)
    value_weight = normal_values(keys[3], (A, C), C ** -0.5, 0.4375)
    post_gain = jnp.clip(1.0 + 0.18 * jax.random.normal(keys[4], (A,), jnp.float32), 0.1, 1.9)
    out_weight = normal_values(keys[5], (C, A), A ** -0.5, 0.5)
    return dict(views=views, conv_weight=conv_weight, match_weight=match_weight, value_weight=value_weight, post_gain=post_gain, out_weight=out_weight)


def latitude_factor(row_total):
    row_index = jnp.arange(row_total, dtype=jnp.int32).astype(jnp.float32)
    latitude = (row_index + 0.5 - 0.5 * row_total) * (2.8 / row_total)
    return 1.0 / (jnp.cos(latitude) + 0.25)

def convolve(views, conv_weight):
    row_count = views.shape[1]
    col_count = views.shape[3]
    padded = jnp.pad(views, ((0, 0), (1, 1), (0, 0), (0, 0)))
    padded = jnp.concatenate([padded[..., -1:], padded, padded[..., :1]], axis=3)
    weight = conv_weight.astype(jnp.float32)
    center = jnp.zeros((2, row_count, conv_weight.shape[1], col_count), jnp.float32)
    side_sum = jnp.zeros((2, row_count, conv_weight.shape[1], col_count), jnp.float32)
    for row_step in range(3):
        for col_step in range(3):
            window = padded[:, row_step:row_step + row_count, :, col_step:col_step + col_count].astype(jnp.float32)
            term = jnp.einsum('oc,vrcw->vrow', weight[3 * row_step + col_step], window, precision=lax.Precision.HIGHEST)
            if col_step == 1:
                center = center + term
            else:
                side_sum = side_sum + term
    side_weight = latitude_factor(row_count)
    return center + side_weight[None, :, None, None] * side_sum

def reference(views, conv_weight, match_weight, value_weight, post_gain, out_weight):
    convolved = convolve(views, conv_weight)
    refined = (views.astype(jnp.float32) + jax.nn.gelu(convolved, approximate=True)).astype(jnp.bfloat16)
    refined_wide = refined.astype(jnp.float32)
    matched = jnp.einsum('ac,vrcw->vraw', match_weight.astype(jnp.float32), refined_wide, precision=lax.Precision.HIGHEST).astype(jnp.bfloat16)
    valued = jnp.einsum('ac,vrcw->vraw', value_weight.astype(jnp.float32), refined_wide, precision=lax.Precision.HIGHEST).astype(jnp.bfloat16)
    score_scale = 1.0 / matched.shape[2] ** 0.5

    def one_row(row_number):
        match_row = lax.dynamic_index_in_dim(matched, row_number, 1, keepdims=False)
        value_row = lax.dynamic_index_in_dim(valued, row_number, 1, keepdims=False)
        refined_row = lax.dynamic_index_in_dim(refined, row_number, 1, keepdims=False)
        results = []
        for query_view in range(2):
            other_view = 1 - query_view
            scores = jnp.dot(match_row[query_view].T, match_row[other_view], preferred_element_type=jnp.float32) * score_scale
            peak = lax.optimization_barrier(jnp.max(scores, axis=1, keepdims=True))
            weights = jnp.exp(scores - peak)
            totals = lax.optimization_barrier(jnp.sum(weights, axis=1))
            numerator = jnp.dot(weights.astype(jnp.bfloat16), value_row[other_view].T, preferred_element_type=jnp.float32)
            attended = numerator / totals[:, None]
            normed = attended * lax.rsqrt(lax.optimization_barrier(jnp.mean(attended * attended, axis=1, keepdims=True)) + 1e-06) * post_gain[None, :]
            delta = jnp.dot(normed.astype(jnp.bfloat16), out_weight.T, preferred_element_type=jnp.float32)
            results.append((refined_row[query_view].astype(jnp.float32) + delta.T).astype(jnp.bfloat16))
        return jnp.stack(results)
    rows_out = lax.map(one_row, jnp.arange(matched.shape[1], dtype=jnp.int32))
    return jnp.transpose(rows_out, (1, 0, 2, 3))
```

```python
import functools
import math

import jax
import jax.numpy as jnp
from jax import lax
from jax.experimental import pallas as pl
from jax.experimental.pallas import tpu as pltpu
from jax.sharding import PartitionSpec as P

F32 = jnp.float32
BF16 = jnp.bfloat16
VMEM_LIMIT = 56 * 1024 * 1024


def conv_kernel(row, side_ref, xu, xm, xd, eu, em, ed, w_ref, out_ref):
    chan = w_ref.shape[1]
    cols = xm.shape[3]
    y = None
    for step, (x, e) in enumerate(((xu, eu), (xm, em), (xd, ed))):
        w = w_ref[3 * step : 3 * step + 3].reshape(3 * chan, chan)
        xe = jnp.concatenate([x[0, 0], e[0, 0]], axis=1)
        term = jnp.dot(w, xe, preferred_element_type=F32)
        y = term if y is None else y + term
    wide = y.shape[1]
    left = pltpu.roll(y[:chan], 1, axis=1)[:, :cols]
    right = pltpu.roll(y[2 * chan :], wide - 1, axis=1)[:, :cols]
    conv = y[chan : 2 * chan, :cols] + side_ref[row] * (left + right)
    out_ref[0, 0] = (xm[0, 0].astype(F32) + jax.nn.gelu(conv, approximate=True)).astype(BF16)


def conv_row(row, side, parts, edges, conv_weight):
    (_, mid_row) = parts[1]
    chan, cols = parts[1][0].shape[2], parts[1][0].shape[3]

    def spec(index, width):
        return pl.BlockSpec((1, 1, chan, width), lambda v: (v, index, 0, 0))

    return pl.pallas_call(
        functools.partial(conv_kernel, row),
        grid=(2,),
        in_specs=[pl.BlockSpec(memory_space=pltpu.SMEM)]
        + [spec(i, cols) for _, i in parts]
        + [spec(i, 128) for _, i in edges]
        + [pl.BlockSpec(conv_weight.shape, lambda v: (0, 0, 0))],
        out_specs=spec(0, cols),
        out_shape=jax.ShapeDtypeStruct((2, 1, chan, cols), BF16),
        compiler_params=pltpu.CompilerParams(vmem_limit_bytes=VMEM_LIMIT),
        cost_estimate=pl.CostEstimate(
            flops=2 * 2 * 9 * chan * chan * cols,
            bytes_accessed=2 * 2 * 4 * chan * cols,
            transcendentals=2 * chan * cols,
        ),
        name="conv_row",
    )(side, *[x for x, _ in parts], *[e for e, _ in edges], conv_weight)


def attend_kernel(count, tj, tk, *refs):
    own = refs[0]
    blocks = refs[1 : 1 + count]
    wkv, gain, ow = refs[1 + count : 4 + count]
    out_ref, kbuf, vbuf, qbuf, acc = refs[5 + count :]
    chan = wkv.shape[0] // 2
    cols = own.shape[3]
    keys = kbuf.shape[1]
    scale = 1.0 / math.sqrt(chan)
    log2e = 1.4426950408889634
    mult = scale * log2e

    kmax = jnp.zeros((1, cols), F32)
    for b, blk in enumerate(blocks):
        kv = jnp.dot(wkv[...], blk[0, 0], preferred_element_type=F32)
        k16 = kv[:chan].astype(BF16)
        kbuf[:, b * cols : (b + 1) * cols] = k16
        kf = k16.astype(F32)
        kmax = jnp.maximum(kmax, jnp.sum(kf * kf, axis=0, keepdims=True))
        vbuf[b * cols : (b + 1) * cols, :chan] = kv[chan:].T.astype(BF16)
    vbuf[:, chan:] = jnp.ones((keys, chan), BF16)
    q = jnp.dot(wkv[:chan], own[0, 0], preferred_element_type=F32)
    qr = q.astype(BF16).astype(F32)
    qmax = jnp.max(jnp.sum(qr * qr, axis=0, keepdims=True))
    qbuf[...] = q.T.astype(BF16)
    bound = jnp.sqrt(qmax) * jnp.sqrt(jnp.max(kmax)) * scale
    small = bound < 60.0

    def finish(j):
        total = acc[...]
        att = total[:, :chan] / total[:, chan:]
        ms = jnp.mean(att * att, axis=1, keepdims=True)
        normed = (att * lax.rsqrt(ms + 1e-06) * gain[...]).astype(BF16)
        delta = lax.dot_general(
            ow[...], normed, (((1,), (1,)), ((), ())), preferred_element_type=F32
        )
        out_ref[0, 0, :, pl.ds(j, tj)] = (
            own[0, 0, :, pl.ds(j, tj)].astype(F32) + delta
        ).astype(BF16)

    @pl.when(small)
    def _():
        @pl.loop(0, cols // tj)
        def _(step):
            j = pl.multiple_of(step * tj, tj)
            qb = qbuf[pl.ds(j, tj), :]
            total = None
            for kc in range(0, keys, tk):
                s = jnp.dot(qb, kbuf[:, kc : kc + tk], preferred_element_type=F32)
                p = jnp.exp2(s * mult).astype(BF16)
                term = jnp.dot(p, vbuf[kc : kc + tk, :], preferred_element_type=F32)
                total = term if total is None else total + term
            acc[...] = total
            finish(j)

    @pl.when(jnp.logical_not(small))
    def _():
        @pl.loop(0, cols // tj)
        def _(step):
            j = pl.multiple_of(step * tj, tj)
            qb = qbuf[pl.ds(j, tj), :]

            def scores(i):
                kc = pl.multiple_of(i * tk, tk)
                return jnp.dot(qb, kbuf[:, pl.ds(kc, tk)], preferred_element_type=F32) * scale

            peak = lax.fori_loop(
                0,
                keys // tk,
                lambda i, m: jnp.maximum(m, jnp.max(scores(i), axis=1, keepdims=True)),
                jnp.full((tj, 1), -jnp.inf, F32),
            )
            acc[...] = jnp.zeros_like(acc)

            @pl.loop(0, keys // tk)
            def _(i):
                p = jnp.exp(scores(i) - peak).astype(BF16)
                kc = pl.multiple_of(i * tk, tk)
                acc[...] += jnp.dot(p, vbuf[pl.ds(kc, tk), :], preferred_element_type=F32)

            finish(j)


def attend_row(row, own, blocks, wkv, gain, ow, out_buf, out_shape):
    chan, cols = own.shape[2], own.shape[3]
    att = gain.shape[1]
    count = len(blocks)
    keys = count * cols
    tj, tk = min(256, cols), 512

    def whole(a):
        return pl.BlockSpec(a.shape, lambda v: (0,) * a.ndim)

    return pl.pallas_call(
        functools.partial(attend_kernel, count, tj, tk),
        grid=(2,),
        in_specs=[pl.BlockSpec((1, 1, chan, cols), lambda v: (v, 0, 0, 0))]
        + [pl.BlockSpec((1, 1, chan, cols), lambda v: (1 - v, 0, 0, 0))] * count
        + [whole(wkv), whole(gain), whole(ow), pl.BlockSpec(memory_space=pl.ANY)],
        out_specs=pl.BlockSpec((1, 1, chan, cols), lambda v: (v, row, 0, 0)),
        out_shape=jax.ShapeDtypeStruct(out_shape, BF16),
        scratch_shapes=[
            pltpu.VMEM((att, keys), BF16),
            pltpu.VMEM((keys, 2 * att), BF16),
            pltpu.VMEM((cols, att), BF16),
            pltpu.VMEM((tj, 2 * att), F32),
        ],
        input_output_aliases={4 + count: 0},
        compiler_params=pltpu.CompilerParams(vmem_limit_bytes=VMEM_LIMIT),
        cost_estimate=pl.CostEstimate(
            flops=2 * 2 * 2 * 2 * cols * keys * att,
            bytes_accessed=2 * 2 * (count + 2) * chan * cols,
            transcendentals=2 * cols * keys,
        ),
        name="attend_row",
    )(own, *blocks, wkv, gain, ow, out_buf)


def body(views, conv_weight, match_weight, value_weight, post_gain, out_weight):
    _, rows, chan, cols = views.shape
    lat, lon = lax.axis_size("lat"), lax.axis_size("lon")
    forward = [(i, (i + 1) % lon) for i in range(lon)]
    backward = [((i + 1) % lon, i) for i in range(lon)]
    down = [(i, i + 1) for i in range(lat - 1)]
    up = [(i + 1, i) for i in range(lat - 1)]
    swap = [(i, i ^ 1) for i in range(lon)]

    from_left = lax.ppermute(views[..., cols - 1], "lon", forward)
    from_right = lax.ppermute(views[..., 0], "lon", backward)
    edges = jnp.concatenate(
        [
            from_right[..., None],
            jnp.zeros((2, rows, chan, 126), BF16),
            from_left[..., None],
        ],
        axis=3,
    )
    top = lax.ppermute(views[:, rows - 1 :], "lat", down)
    bottom = lax.ppermute(views[:, :1], "lat", up)
    edge_top = lax.ppermute(edges[:, rows - 1 :], "lat", down)
    edge_bottom = lax.ppermute(edges[:, :1], "lat", up)

    row_total = rows * lat
    row_index = (lax.axis_index("lat") * rows + jnp.arange(rows, dtype=jnp.int32)).astype(F32)
    latitude = (row_index + 0.5 - 0.5 * row_total) * (2.8 / row_total)
    side = 1.0 / (jnp.cos(latitude) + 0.25)
    wkv = jnp.concatenate([match_weight, value_weight], axis=0)
    gain = post_gain[None, :]

    def source(r, own, first, last):
        if r < 0:
            return (first, 0)
        if r >= rows:
            return (last, 0)
        return (own, r)

    order = list(range(1, rows - 1)) + [0, rows - 1]
    gathered = []
    for r in order:
        parts = [source(r + a, views, top, bottom) for a in (-1, 0, 1)]
        sides = [source(r + a, edges, edge_top, edge_bottom) for a in (-1, 0, 1)]
        own = conv_row(r, side, parts, sides, conv_weight)
        same_core = [own]
        for s in range(1, lon // 2):
            same_core.append(
                lax.ppermute(own, "lon", [(i, (i + 2 * s) % lon) for i in range(lon)])
            )
        other_core = [lax.ppermute(b, "lon", swap) for b in same_core]
        gathered.append((r, own, same_core + other_core))
    out = jnp.zeros(views.shape, BF16)
    for r, own, blocks in gathered:
        out = attend_row(r, own, blocks, wkv, gain, out_weight, out, views.shape)
    return out


def solution(mesh):
    placed = (P(None, "lat", None, "lon"), P(), P(), P(), P(), P())
    return jax.shard_map(
        body, mesh=mesh, in_specs=placed, out_specs=P(None, "lat", None, "lon"), check_vma=False
    )
```

```python
import functools
import math

import jax
import jax.numpy as jnp
from jax import lax
from jax.experimental import pallas as pl
from jax.experimental.pallas import tpu as pltpu
from jax.sharding import PartitionSpec as P

F32 = jnp.float32
BF16 = jnp.bfloat16
VMEM_LIMIT = 56 * 1024 * 1024


def conv_kernel(row, side_ref, xu, xm, xd, eu, em, ed, w_ref, *refs):
    out_ref = refs[-1]
    chan = w_ref.shape[1]
    cols = xm.shape[3]
    w = jnp.concatenate(
        [w_ref[3 * a : 3 * a + 3].reshape(3 * chan, chan) for a in range(3)], axis=1
    )
    xe = jnp.concatenate(
        [jnp.concatenate([x[0, 0], e[0, 0]], axis=1) for x, e in ((xu, eu), (xm, em), (xd, ed))],
        axis=0,
    )
    y = jnp.dot(w, xe, preferred_element_type=F32)
    wide = y.shape[1]
    left = pltpu.roll(y[:chan], 1, axis=1)[:, :cols]
    right = pltpu.roll(y[2 * chan :], wide - 1, axis=1)[:, :cols]
    conv = y[chan : 2 * chan, :cols] + side_ref[row] * (left + right)
    out_ref[0, 0] = (xm[0, 0].astype(F32) + jax.nn.gelu(conv, approximate=True)).astype(BF16)


def conv_row(row, side, parts, edges, conv_weight, after):
    chan, cols = parts[1][0].shape[2], parts[1][0].shape[3]

    def spec(index, width):
        return pl.BlockSpec((1, 1, chan, width), lambda v: (v, index, 0, 0))

    return pl.pallas_call(
        functools.partial(conv_kernel, row),
        grid=(2,),
        in_specs=[pl.BlockSpec(memory_space=pltpu.SMEM)]
        + [spec(i, cols) for _, i in parts]
        + [spec(i, 128) for _, i in edges]
        + [pl.BlockSpec(conv_weight.shape, lambda v: (0, 0, 0))]
        + [pl.BlockSpec(memory_space=pl.ANY) for _ in after],
        out_specs=spec(0, cols),
        out_shape=jax.ShapeDtypeStruct((2, 1, chan, cols), BF16),
        compiler_params=pltpu.CompilerParams(vmem_limit_bytes=VMEM_LIMIT),
        cost_estimate=pl.CostEstimate(
            flops=2 * 2 * 9 * chan * chan * cols,
            bytes_accessed=2 * 2 * 4 * chan * cols,
            transcendentals=2 * chan * cols,
        ),
        name="conv_row",
    )(side, *[x for x, _ in parts], *[e for e, _ in edges], conv_weight, *after)


def attend_kernel(count, tj, tk, *refs):
    own = refs[0]
    blocks = refs[1 : 1 + count]
    wkv, gain, ow = refs[1 + count : 4 + count]
    out_ref, token, kbuf, vbuf, qbuf, acc = refs[5 + count :]
    chan = wkv.shape[0] // 2
    cols = own.shape[3]
    keys = kbuf.shape[0]
    scale = 1.0 / math.sqrt(chan)
    mult = scale * 1.4426950408889634

    token[...] = jnp.zeros_like(token)
    kmax = jnp.zeros((1, cols), F32)
    for b, blk in enumerate(blocks):
        kv = jnp.dot(wkv[...], blk[0, 0], preferred_element_type=F32)
        k16 = kv[:chan].astype(BF16)
        kf = k16.astype(F32)
        kmax = jnp.maximum(kmax, jnp.sum(kf * kf, axis=0, keepdims=True))
        kbuf[b * cols : (b + 1) * cols, :] = k16.T
        vbuf[:chan, b * cols : (b + 1) * cols] = kv[chan:].astype(BF16)
    vbuf[chan:, :] = jnp.ones((16, keys), BF16)
    q16 = jnp.dot(wkv[:chan], own[0, 0], preferred_element_type=F32).astype(BF16)
    qr = q16.astype(F32)
    qmax = jnp.max(jnp.sum(qr * qr, axis=0, keepdims=True))
    qbuf[...] = q16
    bound = jnp.sqrt(qmax) * jnp.sqrt(jnp.max(kmax)) * scale
    small = bound < 60.0

    def finish(j, total):
        att = total[:chan] / total[chan : chan + 1]
        ms = jnp.mean(att * att, axis=0, keepdims=True)
        normed = (att * lax.rsqrt(ms + 1e-06) * gain[...]).astype(BF16)
        delta = jnp.dot(ow[...], normed, preferred_element_type=F32)
        out_ref[0, 0, :, pl.ds(j, tj)] = (
            own[0, 0, :, pl.ds(j, tj)].astype(F32) + delta
        ).astype(BF16)

    @pl.when(small)
    def _():
        @pl.loop(0, cols // tj)
        def _(step):
            j = pl.multiple_of(step * tj, tj)
            qb = qbuf[:, pl.ds(j, tj)]

            def scores(kc):
                return jnp.dot(kbuf[kc : kc + tk, :], qb, preferred_element_type=F32)

            total = None
            ahead = scores(0)
            for kc in range(0, keys, tk):
                s = ahead
                if kc + tk < keys:
                    ahead = scores(kc + tk)
                p = jnp.exp2(s * mult).astype(BF16)
                term = jnp.dot(vbuf[:, kc : kc + tk], p, preferred_element_type=F32)
                total = term if total is None else total + term
            finish(j, total)

    @pl.when(jnp.logical_not(small))
    def _():
        @pl.loop(0, cols // tj)
        def _(step):
            j = pl.multiple_of(step * tj, tj)
            qb = qbuf[:, pl.ds(j, tj)]

            def scores(i):
                kc = pl.multiple_of(i * tk, tk)
                return jnp.dot(kbuf[pl.ds(kc, tk), :], qb, preferred_element_type=F32) * scale

            peak = lax.fori_loop(
                0,
                keys // tk,
                lambda i, m: jnp.maximum(m, jnp.max(scores(i), axis=0, keepdims=True)),
                jnp.full((1, tj), -jnp.inf, F32),
            )
            acc[...] = jnp.zeros_like(acc)

            @pl.loop(0, keys // tk)
            def _(i):
                p = jnp.exp(scores(i) - peak).astype(BF16)
                kc = pl.multiple_of(i * tk, tk)
                acc[...] += jnp.dot(vbuf[:, pl.ds(kc, tk)], p, preferred_element_type=F32)

            finish(j, acc[...])


def attend_row(row, own, blocks, wkv, gain, ow, out_buf, out_shape):
    chan, cols = own.shape[2], own.shape[3]
    att = gain.shape[0]
    count = len(blocks)
    keys = count * cols
    tj, tk = min(1024, cols), 256

    def whole(a):
        return pl.BlockSpec(a.shape, lambda v: (0,) * a.ndim)

    return pl.pallas_call(
        functools.partial(attend_kernel, count, tj, tk),
        grid=(2,),
        in_specs=[pl.BlockSpec((1, 1, chan, cols), lambda v: (v, 0, 0, 0))]
        + [pl.BlockSpec((1, 1, chan, cols), lambda v: (1 - v, 0, 0, 0))] * count
        + [whole(wkv), whole(gain), whole(ow), pl.BlockSpec(memory_space=pl.ANY)],
        out_specs=[
            pl.BlockSpec((1, 1, chan, cols), lambda v: (v, row, 0, 0)),
            pl.BlockSpec((8, 128), lambda v: (0, 0)),
        ],
        out_shape=[
            jax.ShapeDtypeStruct(out_shape, BF16),
            jax.ShapeDtypeStruct((8, 128), F32),
        ],
        scratch_shapes=[
            pltpu.VMEM((keys, att), BF16),
            pltpu.VMEM((att + 16, keys), BF16),
            pltpu.VMEM((att, cols), BF16),
            pltpu.VMEM((att + 16, tj), F32),
        ],
        input_output_aliases={4 + count: 0},
        compiler_params=pltpu.CompilerParams(vmem_limit_bytes=VMEM_LIMIT),
        cost_estimate=pl.CostEstimate(
            flops=2 * 2 * 2 * 2 * cols * keys * att,
            bytes_accessed=2 * 2 * (count + 2) * chan * cols,
            transcendentals=2 * cols * keys,
        ),
        name="attend_row",
    )(own, *blocks, wkv, gain, ow, out_buf)


def body(views, conv_weight, match_weight, value_weight, post_gain, out_weight):
    _, rows, chan, cols = views.shape
    lat, lon = lax.axis_size("lat"), lax.axis_size("lon")
    forward = [(i, (i + 1) % lon) for i in range(lon)]
    backward = [((i + 1) % lon, i) for i in range(lon)]
    down = [(i, i + 1) for i in range(lat - 1)]
    up = [(i + 1, i) for i in range(lat - 1)]
    swap = [(i, i ^ 1) for i in range(lon)]

    last_row, first_row = lax.optimization_barrier((views[:, rows - 1 :], views[:, :1]))
    top = lax.ppermute(last_row, "lat", down)
    bottom = lax.ppermute(first_row, "lat", up)
    from_left = lax.ppermute(views[..., cols - 1], "lon", forward)
    from_right = lax.ppermute(views[..., 0], "lon", backward)
    edges = jnp.concatenate(
        [
            from_right[..., None],
            jnp.zeros((2, rows, chan, 126), BF16),
            from_left[..., None],
        ],
        axis=3,
    )
    edge_top = lax.ppermute(edges[:, rows - 1 :], "lat", down)
    edge_bottom = lax.ppermute(edges[:, :1], "lat", up)

    row_total = rows * lat
    row_index = (lax.axis_index("lat") * rows + jnp.arange(rows, dtype=jnp.int32)).astype(F32)
    latitude = (row_index + 0.5 - 0.5 * row_total) * (2.8 / row_total)
    side = 1.0 / (jnp.cos(latitude) + 0.25)
    wkv = jnp.concatenate([match_weight, value_weight], axis=0)
    gain = post_gain[:, None]

    def source(r, own, first, last):
        if r < 0:
            return (first, 0)
        if r >= rows:
            return (last, 0)
        return (own, r)

    def convolve(r, after):
        parts = [source(r + a, views, top, bottom) for a in (-1, 0, 1)]
        sides = [source(r + a, edges, edge_top, edge_bottom) for a in (-1, 0, 1)]
        return conv_row(r, side, parts, sides, conv_weight, after)

    def gather(own, after):
        far = [
            lax.ppermute(own, "lon", [(i, (i + 2 * s) % lon) for i in range(lon)])
            for s in range(1, lon // 2)
        ]
        near = [lax.ppermute(lax.optimization_barrier((own, after))[0], "lon", swap)]
        held = [lax.optimization_barrier((b, after))[0] for b in far]
        return [own] + far + near + [lax.ppermute(b, "lon", swap) for b in held]

    def attend(out, row):
        r, own, blocks = row
        return attend_row(r, own, blocks, wkv, gain, out_weight, out, views.shape)

    owns = []
    after = (last_row, first_row)
    order = list(range(1, rows - 1)) + [0, rows - 1]
    for r in order:
        if r == 0:
            after = lax.optimization_barrier((after[0], top, bottom))[:1]
        owns.append(convolve(r, after))
        after = (owns[-1],)
    out = jnp.zeros(views.shape, BF16)
    holds = [after, after]
    for i, (r, own) in enumerate(zip(order, owns)):
        out, token = attend(out, (r, own, gather(own, holds[i])))
        holds.append((token,))
    return out


def solution(mesh):
    placed = (P(None, "lat", None, "lon"), P(), P(), P(), P(), P())
    return jax.shard_map(
        body, mesh=mesh, in_specs=placed, out_specs=P(None, "lat", None, "lon"), check_vma=False
    )
```

```python
import functools
import math

import jax
import jax.numpy as jnp
from jax import lax
from jax.experimental import pallas as pl
from jax.experimental.pallas import tpu as pltpu
from jax.sharding import PartitionSpec as P

F32 = jnp.float32
BF16 = jnp.bfloat16
VMEM_LIMIT = 56 * 1024 * 1024


def conv_kernel(row, side_ref, xu, xm, xd, eu, em, ed, w_ref, *refs):
    out_ref = refs[-1]
    chan = w_ref.shape[1]
    cols = xm.shape[3]
    w = jnp.concatenate(
        [w_ref[3 * a : 3 * a + 3].reshape(3 * chan, chan) for a in range(3)], axis=1
    )
    xe = jnp.concatenate(
        [jnp.concatenate([x[0, 0], e[0, 0]], axis=1) for x, e in ((xu, eu), (xm, em), (xd, ed))],
        axis=0,
    )
    y = jnp.dot(w, xe, preferred_element_type=F32)
    wide = y.shape[1]
    left = pltpu.roll(y[:chan], 1, axis=1)[:, :cols]
    right = pltpu.roll(y[2 * chan :], wide - 1, axis=1)[:, :cols]
    conv = y[chan : 2 * chan, :cols] + side_ref[row] * (left + right)
    out_ref[0, 0] = (xm[0, 0].astype(F32) + jax.nn.gelu(conv, approximate=True)).astype(BF16)


def conv_row(row, side, parts, edges, conv_weight, after):
    chan, cols = parts[1][0].shape[2], parts[1][0].shape[3]

    def spec(index, width):
        return pl.BlockSpec((1, 1, chan, width), lambda v: (v, index, 0, 0))

    return pl.pallas_call(
        functools.partial(conv_kernel, row),
        grid=(2,),
        in_specs=[pl.BlockSpec(memory_space=pltpu.SMEM)]
        + [spec(i, cols) for _, i in parts]
        + [spec(i, 128) for _, i in edges]
        + [pl.BlockSpec(conv_weight.shape, lambda v: (0, 0, 0))]
        + [pl.BlockSpec(memory_space=pl.ANY) for _ in after],
        out_specs=spec(0, cols),
        out_shape=jax.ShapeDtypeStruct((2, 1, chan, cols), BF16),
        compiler_params=pltpu.CompilerParams(vmem_limit_bytes=VMEM_LIMIT),
        cost_estimate=pl.CostEstimate(
            flops=2 * 2 * 9 * chan * chan * cols,
            bytes_accessed=2 * 2 * 4 * chan * cols,
            transcendentals=2 * chan * cols,
        ),
        name="conv_row",
    )(side, *[x for x, _ in parts], *[e for e, _ in edges], conv_weight, *after)


def attend_kernel(count, tj, tk, *refs):
    own = refs[0]
    blocks = refs[1 : 1 + count]
    wkv, gain, ow = refs[1 + count : 4 + count]
    out_ref, token, kbuf, vbuf, qbuf, acc = refs[-6:]
    chan = wkv.shape[0] // 2
    cols = own.shape[3]
    keys = kbuf.shape[0]
    scale = 1.0 / math.sqrt(chan)
    mult = scale * 1.4426950408889634

    token[...] = jnp.zeros_like(token)
    kmax = jnp.zeros((1, cols), F32)
    for b, blk in enumerate(blocks):
        kv = jnp.dot(wkv[...], blk[0, 0], preferred_element_type=F32)
        k16 = kv[:chan].astype(BF16)
        kf = k16.astype(F32)
        kmax = jnp.maximum(kmax, jnp.sum(kf * kf, axis=0, keepdims=True))
        kbuf[b * cols : (b + 1) * cols, :] = k16.T
        vbuf[:chan, b * cols : (b + 1) * cols] = kv[chan:].astype(BF16)
    vbuf[chan:, :] = jnp.ones((16, keys), BF16)
    q16 = jnp.dot(wkv[:chan], own[0, 0], preferred_element_type=F32).astype(BF16)
    qr = q16.astype(F32)
    qmax = jnp.max(jnp.sum(qr * qr, axis=0, keepdims=True))
    qbuf[...] = q16
    bound = jnp.sqrt(qmax) * jnp.sqrt(jnp.max(kmax)) * scale
    small = bound < 60.0

    def finish(j, total):
        att = total[:chan] / total[chan : chan + 1]
        ms = jnp.mean(att * att, axis=0, keepdims=True)
        normed = (att * lax.rsqrt(ms + 1e-06) * gain[...]).astype(BF16)
        delta = jnp.dot(ow[...], normed, preferred_element_type=F32)
        out_ref[0, 0, :, pl.ds(j, tj)] = (
            own[0, 0, :, pl.ds(j, tj)].astype(F32) + delta
        ).astype(BF16)

    @pl.when(small)
    def _():
        @pl.loop(0, cols // tj)
        def _(step):
            j = pl.multiple_of(step * tj, tj)
            qb = qbuf[:, pl.ds(j, tj)]

            def scores(kc):
                return jnp.dot(kbuf[kc : kc + tk, :], qb, preferred_element_type=F32)

            total = None
            ahead = scores(0)
            for kc in range(0, keys, tk):
                s = ahead
                if kc + tk < keys:
                    ahead = scores(kc + tk)
                p = jnp.exp2(s * mult).astype(BF16)
                term = jnp.dot(vbuf[:, kc : kc + tk], p, preferred_element_type=F32)
                total = term if total is None else total + term
            finish(j, total)

    @pl.when(jnp.logical_not(small))
    def _():
        @pl.loop(0, cols // tj)
        def _(step):
            j = pl.multiple_of(step * tj, tj)
            qb = qbuf[:, pl.ds(j, tj)]

            def scores(i):
                kc = pl.multiple_of(i * tk, tk)
                return jnp.dot(kbuf[pl.ds(kc, tk), :], qb, preferred_element_type=F32) * scale

            peak = lax.fori_loop(
                0,
                keys // tk,
                lambda i, m: jnp.maximum(m, jnp.max(scores(i), axis=0, keepdims=True)),
                jnp.full((1, tj), -jnp.inf, F32),
            )
            acc[...] = jnp.zeros_like(acc)

            @pl.loop(0, keys // tk)
            def _(i):
                p = jnp.exp(scores(i) - peak).astype(BF16)
                kc = pl.multiple_of(i * tk, tk)
                acc[...] += jnp.dot(vbuf[:, pl.ds(kc, tk)], p, preferred_element_type=F32)

            finish(j, acc[...])


def attend_row(row, own, blocks, wkv, gain, ow, out_buf, out_shape):
    chan, cols = own.shape[2], own.shape[3]
    att = gain.shape[0]
    count = len(blocks)
    keys = count * cols
    tj, tk = min(1024, cols), 256

    def whole(a):
        return pl.BlockSpec(a.shape, lambda v: (0,) * a.ndim)

    return pl.pallas_call(
        functools.partial(attend_kernel, count, tj, tk),
        grid=(2,),
        in_specs=[pl.BlockSpec((1, 1, chan, cols), lambda v: (v, 0, 0, 0))]
        + [pl.BlockSpec((1, 1, chan, cols), lambda v: (1 - v, 0, 0, 0))] * count
        + [whole(wkv), whole(gain), whole(ow)]
        + [pl.BlockSpec(memory_space=pl.ANY) for _ in out_buf],
        out_specs=[
            pl.BlockSpec((1, 1, chan, cols), lambda v: (v, row, 0, 0)),
            pl.BlockSpec((8, 128), lambda v: (0, 0)),
        ],
        out_shape=[
            jax.ShapeDtypeStruct(out_shape, BF16),
            jax.ShapeDtypeStruct((8, 128), F32),
        ],
        scratch_shapes=[
            pltpu.VMEM((keys, att), BF16),
            pltpu.VMEM((att + 16, keys), BF16),
            pltpu.VMEM((att, cols), BF16),
            pltpu.VMEM((att + 16, tj), F32),
        ],
        input_output_aliases={4 + count: 0} if out_buf else {},
        compiler_params=pltpu.CompilerParams(vmem_limit_bytes=VMEM_LIMIT),
        cost_estimate=pl.CostEstimate(
            flops=2 * 2 * 2 * 2 * cols * keys * att,
            bytes_accessed=2 * 2 * (count + 2) * chan * cols,
            transcendentals=2 * cols * keys,
        ),
        name="attend_row",
    )(own, *blocks, wkv, gain, ow, *out_buf)


def body(views, conv_weight, match_weight, value_weight, post_gain, out_weight):
    _, rows, chan, cols = views.shape
    lat, lon = lax.axis_size("lat"), lax.axis_size("lon")
    forward = [(i, (i + 1) % lon) for i in range(lon)]
    backward = [((i + 1) % lon, i) for i in range(lon)]
    down = [(i, i + 1) for i in range(lat - 1)]
    up = [(i + 1, i) for i in range(lat - 1)]
    swap = [(i, i ^ 1) for i in range(lon)]

    last_row, first_row = lax.optimization_barrier((views[:, rows - 1 :], views[:, :1]))
    top = lax.ppermute(last_row, "lat", down)
    bottom = lax.ppermute(first_row, "lat", up)
    from_left = lax.ppermute(views[..., cols - 1], "lon", forward)
    from_right = lax.ppermute(views[..., 0], "lon", backward)
    edges = jnp.concatenate(
        [
            from_right[..., None],
            jnp.zeros((2, rows, chan, 126), BF16),
            from_left[..., None],
        ],
        axis=3,
    )
    edge_top = lax.ppermute(edges[:, rows - 1 :], "lat", down)
    edge_bottom = lax.ppermute(edges[:, :1], "lat", up)

    row_total = rows * lat
    row_index = (lax.axis_index("lat") * rows + jnp.arange(rows, dtype=jnp.int32)).astype(F32)
    latitude = (row_index + 0.5 - 0.5 * row_total) * (2.8 / row_total)
    side = 1.0 / (jnp.cos(latitude) + 0.25)
    wkv = jnp.concatenate([match_weight, value_weight], axis=0)
    gain = post_gain[:, None]

    def source(r, own, first, last):
        if r < 0:
            return (first, 0)
        if r >= rows:
            return (last, 0)
        return (own, r)

    def convolve(r, after):
        parts = [source(r + a, views, top, bottom) for a in (-1, 0, 1)]
        sides = [source(r + a, edges, edge_top, edge_bottom) for a in (-1, 0, 1)]
        return conv_row(r, side, parts, sides, conv_weight, after)

    def gather(own, after):
        far = [
            lax.ppermute(own, "lon", [(i, (i + 2 * s) % lon) for i in range(lon)])
            for s in range(1, lon // 2)
        ]
        near = [lax.ppermute(lax.optimization_barrier((own, after))[0], "lon", swap)]
        held = [lax.optimization_barrier((b, after))[0] for b in far]
        return [own] + far + near + [lax.ppermute(b, "lon", swap) for b in held]

    def attend(out, row):
        r, own, blocks = row
        return attend_row(r, own, blocks, wkv, gain, out_weight, out, views.shape)

    owns = []
    after = (last_row, first_row)
    order = list(range(1, rows - 1)) + [0, rows - 1]
    for r in order[:-2]:
        owns.append(convolve(r, after))
        after = (owns[-1],)
    whole, token = attend((), (order[0], owns[0], gather(owns[0], after + (bottom,))))
    after = (token,)
    for r in order[-2:]:
        owns.append(convolve(r, after))
        after = (owns[-1],)
    for r, own in list(zip(order, owns))[1:]:
        whole, token = attend((whole,), (r, own, gather(own, after)))
        after = (token,)
    return whole


def solution(mesh):
    placed = (P(None, "lat", None, "lon"), P(), P(), P(), P(), P())
    return jax.shard_map(
        body, mesh=mesh, in_specs=placed, out_specs=P(None, "lat", None, "lon"), check_vma=False
    )
```

```python
import functools
import math

import jax
import jax.numpy as jnp
from jax import lax
from jax.experimental import pallas as pl
from jax.experimental.pallas import tpu as pltpu
from jax.sharding import PartitionSpec as P

F32 = jnp.float32
BF16 = jnp.bfloat16
VMEM_LIMIT = 56 * 1024 * 1024


def conv_kernel(row, side_ref, xu, xm, xd, eu, em, ed, w_ref, *refs):
    out_ref = refs[-1]
    chan = w_ref.shape[1]
    cols = xm.shape[3]
    w = jnp.concatenate(
        [w_ref[3 * a : 3 * a + 3].reshape(3 * chan, chan) for a in range(3)], axis=1
    )
    xe = jnp.concatenate(
        [jnp.concatenate([x[0, 0], e[0, 0]], axis=1) for x, e in ((xu, eu), (xm, em), (xd, ed))],
        axis=0,
    )
    y = jnp.dot(w, xe, preferred_element_type=F32)
    wide = y.shape[1]
    left = pltpu.roll(y[:chan], 1, axis=1)[:, :cols]
    right = pltpu.roll(y[2 * chan :], wide - 1, axis=1)[:, :cols]
    conv = y[chan : 2 * chan, :cols] + side_ref[row] * (left + right)
    out_ref[0, 0] = (xm[0, 0].astype(F32) + jax.nn.gelu(conv, approximate=True)).astype(BF16)


def conv_row(row, side, parts, edges, conv_weight, after):
    chan, cols = parts[1][0].shape[2], parts[1][0].shape[3]

    def spec(index, width):
        return pl.BlockSpec((1, 1, chan, width), lambda v: (v, index, 0, 0))

    return pl.pallas_call(
        functools.partial(conv_kernel, row),
        grid=(2,),
        in_specs=[pl.BlockSpec(memory_space=pltpu.SMEM)]
        + [spec(i, cols) for _, i in parts]
        + [spec(i, 128) for _, i in edges]
        + [pl.BlockSpec(conv_weight.shape, lambda v: (0, 0, 0))]
        + [pl.BlockSpec(memory_space=pl.ANY) for _ in after],
        out_specs=spec(0, cols),
        out_shape=jax.ShapeDtypeStruct((2, 1, chan, cols), BF16),
        compiler_params=pltpu.CompilerParams(vmem_limit_bytes=VMEM_LIMIT),
        cost_estimate=pl.CostEstimate(
            flops=2 * 2 * 9 * chan * chan * cols,
            bytes_accessed=2 * 2 * 4 * chan * cols,
            transcendentals=2 * chan * cols,
        ),
        name="conv_row",
    )(side, *[x for x, _ in parts], *[e for e, _ in edges], conv_weight, *after)


def attend_kernel(count, tj, tk, *refs):
    own = refs[0]
    blocks = refs[1 : 1 + count]
    wkv, gain, ow = refs[1 + count : 4 + count]
    out_ref, token, kbuf, vbuf, qbuf, acc = refs[-6:]
    chan = wkv.shape[0] // 2
    cols = own.shape[3]
    keys = kbuf.shape[0]
    scale = 1.0 / math.sqrt(chan)
    mult = scale * 1.4426950408889634

    token[...] = jnp.zeros_like(token)
    kmax = jnp.zeros((1, cols), F32)
    for b, blk in enumerate(blocks):
        kv = jnp.dot(wkv[...], blk[0, 0], preferred_element_type=F32)
        k16 = kv[:chan].astype(BF16)
        kf = k16.astype(F32)
        kmax = jnp.maximum(kmax, jnp.sum(kf * kf, axis=0, keepdims=True))
        kbuf[b * cols : (b + 1) * cols, :] = k16.T
        vbuf[:chan, b * cols : (b + 1) * cols] = kv[chan:].astype(BF16)
    vbuf[chan:, :] = jnp.ones((16, keys), BF16)
    q16 = jnp.dot(wkv[:chan], own[0, 0], preferred_element_type=F32).astype(BF16)
    qr = q16.astype(F32)
    qmax = jnp.max(jnp.sum(qr * qr, axis=0, keepdims=True))
    qbuf[...] = q16
    bound = jnp.sqrt(qmax) * jnp.sqrt(jnp.max(kmax)) * scale
    small = bound < 60.0

    def finish(j, total):
        att = total[:chan] / total[chan : chan + 1]
        ms = jnp.mean(att * att, axis=0, keepdims=True)
        normed = (att * lax.rsqrt(ms + 1e-06) * gain[...]).astype(BF16)
        delta = jnp.dot(ow[...], normed, preferred_element_type=F32)
        out_ref[0, 0, :, pl.ds(j, tj)] = (
            own[0, 0, :, pl.ds(j, tj)].astype(F32) + delta
        ).astype(BF16)

    @pl.when(small)
    def _():
        @pl.loop(0, cols // tj)
        def _(step):
            j = pl.multiple_of(step * tj, tj)
            qb = qbuf[:, pl.ds(j, tj)]

            def scores(kc):
                return jnp.dot(kbuf[kc : kc + tk, :], qb, preferred_element_type=F32)

            total = None
            ahead = scores(0)
            for kc in range(0, keys, tk):
                s = ahead
                if kc + tk < keys:
                    ahead = scores(kc + tk)
                p = jnp.exp2(s * mult).astype(BF16)
                term = jnp.dot(vbuf[:, kc : kc + tk], p, preferred_element_type=F32)
                total = term if total is None else total + term
            finish(j, total)

    @pl.when(jnp.logical_not(small))
    def _():
        @pl.loop(0, cols // tj)
        def _(step):
            j = pl.multiple_of(step * tj, tj)
            qb = qbuf[:, pl.ds(j, tj)]

            def scores(i):
                kc = pl.multiple_of(i * tk, tk)
                return jnp.dot(kbuf[pl.ds(kc, tk), :], qb, preferred_element_type=F32) * scale

            peak = lax.fori_loop(
                0,
                keys // tk,
                lambda i, m: jnp.maximum(m, jnp.max(scores(i), axis=0, keepdims=True)),
                jnp.full((1, tj), -jnp.inf, F32),
            )
            acc[...] = jnp.zeros_like(acc)

            @pl.loop(0, keys // tk)
            def _(i):
                p = jnp.exp(scores(i) - peak).astype(BF16)
                kc = pl.multiple_of(i * tk, tk)
                acc[...] += jnp.dot(vbuf[:, pl.ds(kc, tk)], p, preferred_element_type=F32)

            finish(j, acc[...])


def attend_row(row, own, blocks, wkv, gain, ow, out_buf, out_shape):
    chan, cols = own.shape[2], own.shape[3]
    att = gain.shape[0]
    count = len(blocks)
    keys = count * cols
    tj, tk = min(1024, cols), 256

    def whole(a):
        return pl.BlockSpec(a.shape, lambda v: (0,) * a.ndim)

    return pl.pallas_call(
        functools.partial(attend_kernel, count, tj, tk),
        grid=(2,),
        in_specs=[pl.BlockSpec((1, 1, chan, cols), lambda v: (v, 0, 0, 0))]
        + [pl.BlockSpec((1, 1, chan, cols), lambda v: (1 - v, 0, 0, 0))] * count
        + [whole(wkv), whole(gain), whole(ow)]
        + [pl.BlockSpec(memory_space=pl.ANY) for _ in out_buf],
        out_specs=[
            pl.BlockSpec((1, 1, chan, cols), lambda v: (v, row, 0, 0)),
            pl.BlockSpec((8, 128), lambda v: (0, 0)),
        ],
        out_shape=[
            jax.ShapeDtypeStruct(out_shape, BF16),
            jax.ShapeDtypeStruct((8, 128), F32),
        ],
        scratch_shapes=[
            pltpu.VMEM((keys, att), BF16),
            pltpu.VMEM((att + 16, keys), BF16),
            pltpu.VMEM((att, cols), BF16),
            pltpu.VMEM((att + 16, tj), F32),
        ],
        input_output_aliases={4 + count: 0} if out_buf else {},
        compiler_params=pltpu.CompilerParams(vmem_limit_bytes=VMEM_LIMIT),
        cost_estimate=pl.CostEstimate(
            flops=2 * 2 * 2 * 2 * cols * keys * att,
            bytes_accessed=2 * 2 * (count + 2) * chan * cols,
            transcendentals=2 * cols * keys,
        ),
        name="attend_row",
    )(own, *blocks, wkv, gain, ow, *out_buf)


def body(views, conv_weight, match_weight, value_weight, post_gain, out_weight):
    _, rows, chan, cols = views.shape
    lat, lon = lax.axis_size("lat"), lax.axis_size("lon")
    forward = [(i, (i + 1) % lon) for i in range(lon)]
    backward = [((i + 1) % lon, i) for i in range(lon)]
    down = [(i, i + 1) for i in range(lat - 1)]
    up = [(i + 1, i) for i in range(lat - 1)]
    swap = [(i, i ^ 1) for i in range(lon)]

    last_row, first_row = lax.optimization_barrier((views[:, rows - 1 :], views[:, :1]))
    top = lax.ppermute(last_row, "lat", down)
    bottom = lax.ppermute(first_row, "lat", up)
    from_left = lax.ppermute(views[..., cols - 1], "lon", forward)
    from_right = lax.ppermute(views[..., 0], "lon", backward)
    edges = jnp.concatenate(
        [
            from_right[..., None],
            jnp.zeros((2, rows, chan, 126), BF16),
            from_left[..., None],
        ],
        axis=3,
    )
    edge_top = lax.ppermute(edges[:, rows - 1 :], "lat", down)
    edge_bottom = lax.ppermute(edges[:, :1], "lat", up)

    row_total = rows * lat
    row_index = (lax.axis_index("lat") * rows + jnp.arange(rows, dtype=jnp.int32)).astype(F32)
    latitude = (row_index + 0.5 - 0.5 * row_total) * (2.8 / row_total)
    side = 1.0 / (jnp.cos(latitude) + 0.25)
    wkv = jnp.concatenate([match_weight, value_weight], axis=0)
    gain = post_gain[:, None]

    def source(r, own, first, last):
        if r < 0:
            return (first, 0)
        if r >= rows:
            return (last, 0)
        return (own, r)

    def convolve(r, after):
        parts = [source(r + a, views, top, bottom) for a in (-1, 0, 1)]
        sides = [source(r + a, edges, edge_top, edge_bottom) for a in (-1, 0, 1)]
        return conv_row(r, side, parts, sides, conv_weight, after)

    def gather(own, after):
        far = [
            lax.ppermute(own, "lon", [(i, (i + 2 * s) % lon) for i in range(lon)])
            for s in range(1, lon // 2)
        ]
        near = [lax.ppermute(lax.optimization_barrier((own, after))[0], "lon", swap)]
        held = [lax.optimization_barrier((b, after))[0] for b in far]
        return [own] + far + near + [lax.ppermute(b, "lon", swap) for b in held]

    def attend(out, row):
        r, own, blocks = row
        return attend_row(r, own, blocks, wkv, gain, out_weight, out, views.shape)

    owns = []
    after = (last_row, first_row)
    order = list(range(1, rows - 1)) + [0, rows - 1]
    for r in order:
        if r == 0:
            after = lax.optimization_barrier((after[0], top, bottom))[:1]
        owns.append(convolve(r, after))
        after = (owns[-1],)
    out = ()
    holds = [after, after]
    for i, (r, own) in enumerate(zip(order, owns)):
        whole, token = attend(out, (r, own, gather(own, holds[i])))
        out = (whole,)
        holds.append((token,))
    return out[0]


def solution(mesh):
    placed = (P(None, "lat", None, "lon"), P(), P(), P(), P(), P())
    return jax.shard_map(
        body, mesh=mesh, in_specs=placed, out_specs=P(None, "lat", None, "lon"), check_vma=False
    )
```
